256 devices in a mesh: dp: 64 (over z, y, core), head: 4 (over x).
Axes of the slice: x: 4, y: 4, z: 8, core: 2. Of those that a mesh axis runs over, the one named last changes fastest.
Arguments:
- tokens: bfloat16 [32768, 2048], P(('dp', 'head')), may hold values from -6 to 6
- routes: int32 [32768, 2], P(('dp', 'head')), may hold values from 0 to 63, all different within a row; in each aligned block of 128 rows (0 to 127, 128 to 255, ...) at most 5 rows name the same one
- lengths: int32 [512], P('dp'), may hold values from 1 to 64, 20480 in all
- moe_gain: float32 [2048], replicated, may hold values from 0.5 to 1.5
- router: bfloat16 [2048, 64], replicated, may hold values from -0.125 to 0.125
- expert_in: bfloat16 [64, 2048, 4096], P('dp', None, 'head'), may hold values from -0.125 to 0.125
- expert_out: bfloat16 [64, 4096, 2048], P('dp', 'head'), may hold values from -0.09375 to 0.09375
- final_gain: float32 [2048], replicated, may hold values from 0.5 to 1.5
- w_query: bfloat16 [2048, 1024], P(None, 'head'), may hold values from -0.125 to 0.125
- w_key: bfloat16 [2048, 1024], P(None, 'head'), may hold values from -0.125 to 0.125
- w_value: bfloat16 [2048, 1024], P(None, 'head'), may hold values from -0.125 to 0.125
- w_output: bfloat16 [1024, 2048], P('head'), may hold values from -0.1875 to 0.1875
- dec_gain: float32 [2048], replicated, may hold values from 0.5 to 1.5
- dec_state: bfloat16 [512, 2048], P('dp'), may hold values from -6 to 6
Outputs:
- decoded: bfloat16 [2, 512, 2048], P(None, 'dp')
The draws below stay inside these ranges and needn't reach their ends.
Inputs may be any that keep to these rules, and one draw needn't show every extreme that they name: `routes`: each row names two different experts. Among the 128 rows of one device (aligned blocks), no expert is named by more than 5 rows, and some block names some expert exactly 5 times. `lengths`: some sentence fills all 64 slots.
All inputs are finite; a program needn't handle non-finite values. No bound on the sum of `lengths` on one device may be relied on, other than what follows from the above.
Results may differ from the reference program's by a relative error of at most 0.015.
Values may be sent and summed in bfloat16 or wider, within the bound.
No kernel may reach another device: no remote copies, remote signals or barrier semaphores. Data moves between devices by JAX's collectives and lax.ppermute only.
A program may use at most 128 MiB of HBM per device.

```python
import math
import jax
import jax.numpy as jnp
import numpy as np
from jax import lax

D = 2048
FF = 4096
HEADS = 8
HD = 128
SLEN = 64
STEPS = 2
TOK_DEV = 128
EXPERTS = 64
CAP = 5
TOKENS = 32768
SENTENCES = 512
N_HEAD = 4


def block_scale(rng, dims, split, least, largest):
    def one(position, blocks):
        heights = jax.random.uniform(jax.random.fold_in(jax.random.fold_in(rng, 6), position), (blocks,), jnp.float32, least / len(split), largest / len(split))
        return jnp.repeat(jnp.exp(heights), dims[position] // blocks).reshape((-1,) + (1,) * (len(dims) - position - 1))

    level = one(*split[0])
    for cut in split[1:]:
        level = level * one(*cut)
    return level


def split_up(count, total, bound, slope):
    loads = [(1 << 20) // math.isqrt(standing ** slope) + 1 for standing in range(2, count + 1)]
    spare, given = total - bound - (count - 1), [1] * (count - 1)
    while spare > 0:
        movable = [i for i in range(count - 1) if given[i] < bound]
        pool, remaining = sum([loads[i] for i in movable]), spare
        for i in movable:
            more = min(bound - given[i], max(1, remaining * loads[i] // pool), spare)
            given[i] = given[i] + more
            spare = spare - more
    return np.array([bound] + given)


def uneven(key, count, total, reach, lean):
    if count == 2:
        one = jax.random.randint(key, (), max(1, total - reach), min(reach, total - 1) + 1)
        return jnp.stack([one, total - one])
    tallies = jnp.asarray(split_up(count, total, reach, lean), jnp.int32)
    pairs = (count - 1) // 2
    source_of, sink = tallies[1:1 + 2 * pairs:2], tallies[2:2 + 2 * pairs:2]
    room = jnp.minimum(source_of - 1, reach - sink)
    shifted = jax.random.randint(jax.random.fold_in(key, 1), (pairs,), 0, 1 << 20) % (room + 1)
    tallies = tallies.at[1:1 + 2 * pairs:2].set(source_of - shifted).at[2:2 + 2 * pairs:2].set(sink + shifted)
    return tallies[jax.random.permutation(jax.random.fold_in(key, 2), count)]


def assign_block(own_key, own, number, rows, amount, top, reach, slope):
    ranking = jax.random.permutation(own_key, amount)
    packed, common = shares(amount, rows * top, reach, slope, True), shares(amount, rows * top, reach, slope, False)
    places = jnp.arange(amount)

    def named(tallies, offset_by):
        used = int((tallies > 0).sum())
        fixed = max(1, used // 4)
        shifted = fixed + (places - fixed + offset_by * (used - fixed)) % max(1, amount - fixed)
        return jnp.zeros((amount,), jnp.int32).at[ranking[jnp.where(places < fixed, places, shifted)]].set(jnp.asarray(tallies, jnp.int32))

    tallies = jnp.where(number % 4 == 0, named(packed, number // 4), named(common, number - number // 4 - 1))
    mixed = jax.random.permutation(jax.random.fold_in(own, 3), amount)
    source_of, sink = mixed[0:amount // 2 * 2:2], mixed[1:amount // 2 * 2:2]
    margin = jnp.minimum(tallies[source_of] - 1, reach - tallies[sink]) // 2
    margin = jnp.where((source_of == ranking[0]) | (sink == ranking[0]) | (tallies[sink] == 0), 0, jnp.maximum(margin, 0))
    shifted = jax.random.randint(jax.random.fold_in(own, 4), (amount // 2,), 0, 1 << 20) % (margin + 1)
    tallies = tallies.at[source_of].add(-shifted).at[sink].add(shifted)
    items = jnp.searchsorted(jnp.cumsum(tallies), jnp.arange(rows * top), side="right").astype(jnp.int32)
    grid = items.reshape(top, rows).T
    grid = grid[jax.random.permutation(jax.random.fold_in(own, 1), rows)]
    offset_by = jax.random.randint(jax.random.fold_in(own, 2), (rows, 1), 0, top)
    return jnp.take_along_axis(grid, (jnp.arange(top)[None, :] + offset_by) % top, axis=1)


def shares(count, total, bound, lean, full):
    weights = [(1 << 20) // math.isqrt(grade ** lean) + 1 for grade in range(1, count + 1)]
    largest = bound if full else min(bound, max(-(-total // count), total * weights[0] // sum(weights)))
    least = 1 if total - largest >= count - 1 else 0
    holding, surplus = [largest] + [least] * (count - 1), total - largest - least * (count - 1)
    while surplus > 0:
        movable = [i for i in range(1, count) if holding[i] < largest] or [i for i in range(1, count) if holding[i] < bound]
        whole, left = sum([weights[i] for i in movable]), surplus
        for i in movable:
            extra = min(bound - holding[i], max(1, left * weights[i] // whole), surplus)
            holding[i] = holding[i] + extra
            surplus = surplus - extra
    return np.array(holding)


def normal_values(stream_key, dims, scale, reach, split=(), kind=jnp.bfloat16):
    loudness = block_scale(stream_key, dims, split, -0.22, 0.18) if split else 1.0
    values = jax.random.normal(stream_key, dims, jnp.float32) * scale * loudness
    return jnp.minimum(jnp.maximum(values, -reach), reach).astype(kind)


def setup_inputs(seed: int = 0) -> dict:
    streams_of = jax.random.split(jax.random.key(seed), 15)
    tokens = normal_values(streams_of[0], (TOKENS, D), 1.0, 6.0, ((0, 256),))
    routes_keys = jax.random.split(jax.random.fold_in(streams_of[1], 1), TOKENS // TOK_DEV)
    routes_turns = jax.random.permutation(jax.random.fold_in(streams_of[1], 3), TOKENS // TOK_DEV)
    routes = jax.vmap(lambda own, number: assign_block(jax.random.fold_in(streams_of[1], 2), own, number, TOK_DEV, EXPERTS, 2, CAP, 2))(routes_keys, routes_turns).reshape((TOKENS, 2))
    lengths = uneven(streams_of[2], SENTENCES, SENTENCES * SLEN * 5 // 8, SLEN, 0).astype(jnp.int32)
    moe_gain = jnp.clip(1.0 + 0.1 * jax.random.normal(streams_of[3], (D,), jnp.float32), 0.5, 1.5)
    router = normal_values(streams_of[4], (D, EXPERTS), D ** -0.5, 0.125)
    expert_in = normal_values(streams_of[5], (EXPERTS, D, FF), D ** -0.5, 0.125, ((0, 64), (2, 4)))
    expert_out = normal_values(streams_of[6], (EXPERTS, FF, D), FF ** -0.5, 0.09375, ((0, 64), (1, 4)))
    final_gain = jnp.clip(1.0 + 0.1 * jax.random.normal(streams_of[7], (D,), jnp.float32), 0.5, 1.5)
    w_query = normal_values(streams_of[8], (D, HEADS * HD), D ** -0.5, 0.125, ((1, 4),))
    w_key = normal_values(streams_of[9], (D, HEADS * HD), D ** -0.5, 0.125, ((1, 4),))
    w_value = normal_values(streams_of[10], (D, HEADS * HD), D ** -0.5, 0.125, ((1, 4),))
    w_output = normal_values(streams_of[11], (HEADS * HD, D), (HEADS * HD) ** -0.5, 0.1875, ((0, 4),))
    dec_gain = jnp.clip(1.0 + 0.1 * jax.random.normal(streams_of[12], (D,), jnp.float32), 0.5, 1.5)
    dec_state = normal_values(streams_of[13], (SENTENCES, D), 1.0, 6.0, ((0, 64),))
    return dict(tokens=tokens, routes=routes, lengths=lengths, moe_gain=moe_gain, router=router, expert_in=expert_in, expert_out=expert_out, final_gain=final_gain, w_query=w_query, w_key=w_key, w_value=w_value, w_output=w_output, dec_gain=dec_gain, dec_state=dec_state)


EPS = 1e-05

def norm_rows(rows, gain):
    mean = lax.optimization_barrier(jnp.mean(rows, axis=-1, keepdims=True))
    centred = rows - mean
    spread = lax.optimization_barrier(jnp.mean(centred * centred, axis=-1, keepdims=True))
    return centred * lax.rsqrt(spread + EPS) * gain.astype(jnp.float32)

def place_rows(routes_block):
    expert_ids = jnp.arange(EXPERTS, dtype=jnp.int32)
    flat = routes_block.reshape(-1)
    hits = (flat[:, None] == expert_ids[None, :]).astype(jnp.int32)
    running = jnp.cumsum(hits, axis=0) - 1
    slots = lax.optimization_barrier(jnp.sum(hits * running, axis=1))
    return slots.reshape(routes_block.shape).astype(jnp.int32)

def reference(tokens, routes, lengths, moe_gain, router, expert_in, expert_out, final_gain, w_query, w_key, w_value, w_output, dec_gain, dec_state):
    blocks = TOKENS // TOK_DEV
    group = FF // N_HEAD
    xf = tokens.astype(jnp.float32)
    normed = norm_rows(xf, moe_gain).astype(jnp.bfloat16)
    logits = jnp.dot(normed, router, preferred_element_type=jnp.float32)
    chosen = jnp.take_along_axis(logits, routes, axis=1)
    first = jax.nn.sigmoid(chosen[:, 0] - chosen[:, 1])
    gates = jnp.stack([first, 1.0 - first], axis=1)
    slots = jax.vmap(place_rows)(routes.reshape(blocks, TOK_DEV, 2)).reshape(TOKENS, 2)
    token_ids = jnp.broadcast_to(jnp.arange(TOKENS, dtype=jnp.int32)[:, None], (TOKENS, 2))
    block_ids = (token_ids // TOK_DEV).astype(jnp.int32)
    table = jnp.full((EXPERTS, blocks, CAP), TOKENS, jnp.int32).at[routes, block_ids, slots].set(token_ids)
    gate_table = jnp.zeros((EXPERTS, blocks, CAP), jnp.float32).at[routes, block_ids, slots].set(gates)
    padded = jnp.concatenate([normed, jnp.zeros((1, D), jnp.bfloat16)], axis=0)

    def one_expert(total, inputs):
        index, weight, first_proj, second_proj = inputs
        flat_index = index.reshape(-1)
        rows = padded[flat_index]
        hidden = jnp.maximum(jnp.dot(rows, first_proj, preferred_element_type=jnp.float32), 0.0).astype(jnp.bfloat16)
        count = hidden.shape[0]
        parts = jnp.einsum('rqf,qfd->qrd', hidden.reshape(count, N_HEAD, group).astype(jnp.float32), second_proj.reshape(N_HEAD, group, D).astype(jnp.float32))
        rounded = lax.optimization_barrier(parts.astype(jnp.bfloat16))
        result = lax.optimization_barrier(jnp.sum(rounded.astype(jnp.float32), axis=0)).astype(jnp.bfloat16)
        total = total.at[flat_index].add(weight.reshape(-1, 1) * result.astype(jnp.float32), mode='drop')
        return (total, None)
    moe, unused = lax.scan(one_expert, jnp.zeros((TOKENS, D), jnp.float32), (table, gate_table, expert_in, expert_out))
    memory = norm_rows(xf + moe, final_gain).astype(jnp.bfloat16)
    keys = jnp.dot(memory, w_key, preferred_element_type=jnp.float32).astype(jnp.bfloat16).reshape(SENTENCES, SLEN, HEADS, HD)
    values = jnp.dot(memory, w_value, preferred_element_type=jnp.float32).astype(jnp.bfloat16).reshape(SENTENCES, SLEN, HEADS, HD)
    valid = jnp.arange(SLEN, dtype=jnp.int32)[None, :] < lengths[:, None]
    state = dec_state
    results = []
    for step in range(STEPS):
        normed_state = norm_rows(state.astype(jnp.float32), dec_gain).astype(jnp.bfloat16)
        query = (jnp.dot(normed_state, w_query, preferred_element_type=jnp.float32) * HD ** (-0.5)).astype(jnp.bfloat16).reshape(SENTENCES, HEADS, HD)
        scores = jnp.einsum('shd,sthd->sht', query.astype(jnp.float32), keys.astype(jnp.float32))
        scores = jnp.where(valid[:, None, :], scores, -1e+30)
        top = lax.optimization_barrier(jnp.max(scores, axis=2, keepdims=True))
        raised = jnp.exp(scores - top)
        probs = (raised / lax.optimization_barrier(jnp.sum(raised, axis=2, keepdims=True))).astype(jnp.bfloat16)
        attended = jnp.einsum('sht,sthd->shd', probs.astype(jnp.float32), values.astype(jnp.float32)).astype(jnp.bfloat16).reshape(SENTENCES, HEADS * HD)
        update = jnp.dot(attended, w_output, preferred_element_type=jnp.float32)
        state = (state.astype(jnp.float32) + update).astype(jnp.bfloat16)
        results.append(state)
    return jnp.stack(results)
```

```python
import jax
import jax.numpy as jnp
from jax import lax
from jax.sharding import PartitionSpec as P

HD = 128
STEPS = 2
EPS = 1e-05
SLOTS = ((0, 1, 2), (3, 4))


def norm_rows(rows, gain):
    mean = jnp.mean(rows, axis=-1, keepdims=True)
    centred = rows - mean
    spread = jnp.mean(centred * centred, axis=-1, keepdims=True)
    return centred * lax.rsqrt(spread + EPS) * gain


def shift(rows, by):
    n = lax.axis_size("head")
    return lax.ppermute(rows, "head", [(i, (i + by) % n) for i in range(n)])


def exchange(rows, experts):
    count, width = rows.shape
    packed = rows.reshape(experts, count // experts * (width // 128), 128)
    moved = lax.all_to_all(packed, "dp", split_axis=0, concat_axis=0, tiled=True)
    return moved.reshape(count, width)


def gather_ring(rows):
    half = rows.shape[0] // 2
    left = shift(rows, 1)
    right = shift(rows, -1)
    top = shift(left[:half], 1)
    bottom = shift(right[half:], -1)
    return rows, left, right, (top, bottom)


def scatter_ring(own, left, right, top, bottom):
    half = own.shape[0] // 2
    f32 = jnp.float32
    from_left = shift(top, 1).astype(f32)
    from_right = shift(bottom, -1).astype(f32)
    to_right = jnp.concatenate([(right[:half].astype(f32) + from_left).astype(jnp.bfloat16), right[half:]])
    to_left = jnp.concatenate([left[:half], (left[half:].astype(f32) + from_right).astype(jnp.bfloat16)])
    a = shift(to_right, 1).astype(f32)
    b = shift(to_left, -1).astype(f32)
    return (own.astype(f32) + a + b).astype(jnp.bfloat16)


def ring_sum(rows):
    f32 = jnp.float32
    others = [shift(rows, by) for by in (1, -1, 2)]
    total = rows.astype(f32)
    for other in others:
        total = total + other.astype(f32)
    return total


def local(
    tokens,
    routes,
    lengths,
    moe_gain,
    router,
    expert_in,
    expert_out,
    final_gain,
    w_query,
    w_key,
    w_value,
    w_output,
    dec_gain,
    dec_state,
):
    experts = lax.axis_size("dp")
    tok_rows, width = tokens.shape
    f32, bf16 = jnp.float32, jnp.bfloat16
    xf = tokens.astype(f32)
    normed = norm_rows(xf, moe_gain).astype(bf16)
    expert_ids = jnp.arange(experts, dtype=jnp.int32)
    hit0 = routes[:, 0:1] == expert_ids[None, :]
    hit1 = routes[:, 1:2] == expert_ids[None, :]
    hits = (hit0 | hit1).astype(bf16)
    row_ids = jnp.arange(tok_rows, dtype=jnp.int32)
    earlier = (row_ids[:, None] > row_ids[None, :]).astype(bf16)
    prior = jnp.dot(earlier, hits, preferred_element_type=f32)

    def ffn(rows):
        hidden = jnp.maximum(jnp.dot(rows, expert_in[0], preferred_element_type=f32), 0.0).astype(bf16)
        return jnp.dot(hidden, expert_out[0], preferred_element_type=f32).astype(bf16)

    answers = []
    for slots in SLOTS:
        ids = jnp.asarray(slots, f32)
        there = prior[:, :, None] == ids[None, None, :]
        placing = ((hits > 0)[:, :, None] & there).astype(bf16).reshape(tok_rows, -1)
        outgoing = lax.dot_general(
            placing, normed, (((0,), (0,)), ((), ())), preferred_element_type=f32
        ).astype(bf16)
        arrived = exchange(outgoing, experts)
        own, left, right, (top, bottom) = gather_ring(arrived)
        answer = scatter_ring(ffn(own), ffn(left), ffn(right), ffn(top), ffn(bottom))
        returned = exchange(answer, experts)
        answers.append((there, returned))

    logits = jnp.dot(normed, router, preferred_element_type=f32)
    chosen0 = jnp.sum(jnp.where(hit0, logits, 0.0), axis=1)
    chosen1 = jnp.sum(jnp.where(hit1, logits, 0.0), axis=1)
    first = jax.nn.sigmoid(chosen0 - chosen1)
    second = 1.0 - first
    mixed_rows = xf
    for hit, gate in ((hit0, first), (hit1, second)):
        picked = 0.0
        for there, returned in answers:
            picking = (hit[:, :, None] & there).astype(bf16).reshape(tok_rows, -1)
            picked = picked + jnp.dot(picking, returned, preferred_element_type=f32)
        mixed_rows = mixed_rows + gate[:, None] * picked
    memory = norm_rows(mixed_rows, final_gain).astype(bf16)
    local_cols = w_key.shape[1]
    joined = jnp.concatenate([w_key, w_value], axis=1)
    projected = jnp.dot(
        lax.all_gather(memory, "head", axis=0, tiled=True),
        joined,
        preferred_element_type=f32,
    ).astype(bf16)
    keys = projected[:, :local_cols]
    values = projected[:, local_cols:]
    sentences = dec_state.shape[0]
    span = keys.shape[0] // sentences
    local_heads = local_cols // HD
    keys_split = keys.reshape(sentences, span, local_heads, HD)
    values_split = values.reshape(sentences, span, local_heads, HD)
    valid = jnp.arange(span, dtype=jnp.int32)[None, :] < lengths[:, None]
    state = dec_state
    results = []
    for step in range(STEPS):
        normed_state = norm_rows(state.astype(f32), dec_gain).astype(bf16)
        query = (
            (jnp.dot(normed_state, w_query, preferred_element_type=f32) * HD ** (-0.5))
            .astype(bf16)
            .reshape(sentences, local_heads, HD)
        )
        scores = jnp.einsum("shd,sthd->sht", query, keys_split, preferred_element_type=f32)
        scores = jnp.where(valid[:, None, :], scores, -1e30)
        top = jnp.max(scores, axis=2, keepdims=True)
        raised = jnp.exp(scores - top)
        probs = (raised / jnp.sum(raised, axis=2, keepdims=True)).astype(bf16)
        attended = (
            jnp.einsum("sht,sthd->shd", probs, values_split, preferred_element_type=f32)
            .astype(bf16)
            .reshape(sentences, local_cols)
        )
        partial_update = jnp.dot(attended, w_output, preferred_element_type=f32).astype(bf16)
        total_update = ring_sum(partial_update)
        state = (state.astype(f32) + total_update).astype(bf16)
        results.append(state)
    return jnp.stack(results)


def solution(mesh):
    in_specs = (
        P(("dp", "head"), None),
        P(("dp", "head"), None),
        P("dp"),
        P(),
        P(),
        P("dp", None, "head"),
        P("dp", "head", None),
        P(),
        P(None, "head"),
        P(None, "head"),
        P(None, "head"),
        P("head", None),
        P(),
        P("dp", None),
    )
    out_specs = P(None, "dp", None)
    return jax.shard_map(local, mesh=mesh, in_specs=in_specs, out_specs=out_specs, check_vma=False)
```

```python
import functools

import jax
import jax.numpy as jnp
from jax import lax
from jax.experimental import pallas as pl
from jax.experimental.pallas import tpu as pltpu
from jax.sharding import PartitionSpec as P

HD = 128
STEPS = 2
ROOM = (128, 112)
EPS = 1e-05
SLOTS = (0, 1, 2, 3, 4)


def norm_rows(rows, gain):
    mean = jnp.mean(rows, axis=-1, keepdims=True)
    centred = rows - mean
    spread = jnp.mean(centred * centred, axis=-1, keepdims=True)
    return centred * lax.rsqrt(spread + EPS) * gain


def shift(rows, by):
    n = lax.axis_size("head")
    return lax.ppermute(rows, "head", [(i, (i + by) % n) for i in range(n)])


def exchange(rows, experts):
    count, width = rows.shape
    packed = rows.reshape(experts, count // experts * (width // 128), 128)
    return lax.all_to_all(packed, "dp", split_axis=0, concat_axis=0, tiled=True)


def ffn_kernel(count, *refs):
    ins, w_in, w_out, outs = refs[:count], refs[count], refs[count + 1], refs[count + 2 : 2 * count + 2]
    flag, rows, total = refs[2 * count + 2 :]
    step = pl.program_id(0)
    starts = []
    at = 0
    for ref in ins:
        starts.append((at, ref.shape[0]))
        at += ref.shape[0]

    @pl.when(step == 0)
    def _():
        for ref, (start, size) in zip(ins, starts):
            rows[start : start + size, :] = ref[...]
        last = rows[at - 16 : at, 0:128].astype(jnp.float32)
        is_last = lax.broadcasted_iota(jnp.int32, last.shape, 0) == 15
        flag[0, 0] = jnp.max(jnp.where(is_last, last, 0.0)).astype(jnp.int32)

    hidden = jnp.maximum(jnp.dot(rows[...], w_in[0], preferred_element_type=jnp.float32), 0.0).astype(jnp.bfloat16)
    part = jnp.dot(hidden, w_out[0], preferred_element_type=jnp.float32)

    @pl.when(step == 0)
    def _():
        total[...] = part

    @pl.when(step > 0)
    def _():
        total[...] += part

    @pl.when(step == pl.num_programs(0) - 1)
    def _():
        for ref, (start, size) in zip(outs, starts):
            ref[...] = total[start : start + size, :].astype(jnp.bfloat16)


def ffn(blocks, expert_in, expert_out):
    width, units = expert_in.shape[1:]
    tile = 512
    total = sum(block.shape[0] for block in blocks)
    whole = [pl.BlockSpec(block.shape, lambda i: (0, 0)) for block in blocks]
    *shares, flag = pl.pallas_call(
        functools.partial(ffn_kernel, len(blocks)),
        grid=(units // tile,),
        out_shape=[jax.ShapeDtypeStruct(block.shape, jnp.bfloat16) for block in blocks]
        + [jax.ShapeDtypeStruct((1, 1), jnp.int32)],
        in_specs=whole
        + [
            pl.BlockSpec((1, width, tile), lambda i: (0, 0, i)),
            pl.BlockSpec((1, tile, width), lambda i: (0, i, 0)),
        ],
        out_specs=whole + [pl.BlockSpec(memory_space=pltpu.SMEM)],
        scratch_shapes=[pltpu.VMEM((total, width), jnp.bfloat16), pltpu.VMEM((total, width), jnp.float32)],
        compiler_params=pltpu.CompilerParams(vmem_limit_bytes=30 << 20),
        cost_estimate=pl.CostEstimate(
            flops=4 * total * width * units, bytes_accessed=4 * width * units + 4 * total * width, transcendentals=0
        ),
    )(*blocks, expert_in, expert_out)
    return shares, flag[0, 0]


def ring_blocks(rows):
    return [rows] + [shift(rows, by) for by in (1, -1, 2)]


def few_through_experts(blocks, expert_in, expert_out):
    shares, unused = ffn(blocks, expert_in, expert_out)
    total = shares[0].astype(jnp.float32)
    for share, by in zip(shares[1:], (-1, 1, -2)):
        total = total + shift(share, by).astype(jnp.float32)
    return total.astype(jnp.bfloat16)


def pack(rows):
    count = rows.shape[0]
    used = jnp.max(jnp.abs(rows), axis=1) > 0
    ids = jnp.arange(count, dtype=jnp.int32)
    earlier = (ids[:, None] > ids[None, :]).astype(jnp.bfloat16)
    place = jnp.dot(earlier, used.astype(jnp.bfloat16)[:, None], preferred_element_type=jnp.float32)[:, 0]
    place = jnp.where(used, place, -1.0)
    top, bottom = ROOM
    front = top + bottom - 1
    rest = -(-(count - front) // 16) * 16
    places = []
    for start, size, valid in ((0, top, top), (top, bottom, bottom - 1), (front, rest, rest)):
        ids = jnp.arange(size, dtype=jnp.float32)
        ids = jnp.where(ids < valid, ids + start, -2.0)
        places.append((ids[:, None] == place[None, :]).astype(jnp.bfloat16))
    return places, jnp.sum(used.astype(jnp.float32))


def select(places, rows):
    return jnp.dot(places, rows, preferred_element_type=jnp.float32).astype(jnp.bfloat16)


def spread(places, rows):
    return lax.dot_general(places, rows, (((0,), (0,)), ((), ())), preferred_element_type=jnp.float32)


def add(*terms):
    return functools.reduce(lambda a, b: a + b, [term.astype(jnp.float32) for term in terms]).astype(jnp.bfloat16)


def through_experts(top, bottom, crowded, rest_of, expert_in, expert_out):
    left_top, right_bottom = shift(top, 1), shift(bottom, -1)
    left_bottom, right_top = shift(bottom, 1), shift(top, -1)
    far_top, far_bottom = shift(left_top, 1), shift(right_bottom, -1)
    (for_left_top, for_right_bottom), flag1 = ffn((left_top, right_bottom), expert_in, expert_out)
    far_top, far_bottom, for_left_top, for_right_bottom = lax.optimization_barrier(
        (far_top, far_bottom, for_left_top, for_right_bottom)
    )
    (for_far_top, for_far_bottom), flag2 = ffn((far_top, far_bottom), expert_in, expert_out)
    passing_top, passing_bottom = shift(for_far_top, 1), shift(for_far_bottom, -1)
    right_top, left_bottom, for_far_top, for_far_bottom = lax.optimization_barrier(
        (right_top, left_bottom, for_far_top, for_far_bottom)
    )
    (for_right_top, for_left_bottom), flag3 = ffn((right_top, left_bottom), expert_in, expert_out)
    a_bottom, b_top = shift(for_right_bottom, 1), shift(for_left_top, -1)
    a_top = shift(add(for_right_top, passing_top), 1)
    b_bottom = shift(add(for_left_bottom, passing_bottom), -1)
    rest = rest_of((crowded + flag1 + flag2 + flag3) > 0)
    top, bottom, rest = lax.optimization_barrier((top, bottom, rest))
    (own_top, own_bottom), unused = ffn((top, bottom), expert_in, expert_out)
    return add(own_top, a_top, b_top), add(own_bottom, a_bottom, b_bottom), rest


def ring_sum(rows):
    f32 = jnp.float32
    others = [shift(rows, by) for by in (1, -1, 2)]
    total = rows.astype(f32)
    for other in others:
        total = total + other.astype(f32)
    return total


def local(
    tokens,
    routes,
    lengths,
    moe_gain,
    router,
    expert_in,
    expert_out,
    final_gain,
    w_query,
    w_key,
    w_value,
    w_output,
    dec_gain,
    dec_state,
):
    experts = lax.axis_size("dp")
    tok_rows, width = tokens.shape
    f32, bf16 = jnp.float32, jnp.bfloat16
    xf = tokens.astype(f32)
    normed = norm_rows(xf, moe_gain).astype(bf16)
    expert_ids = jnp.arange(experts, dtype=jnp.int32)
    hit0 = routes[:, 0:1] == expert_ids[None, :]
    hit1 = routes[:, 1:2] == expert_ids[None, :]
    row_ids = jnp.arange(tok_rows, dtype=jnp.int32)
    span = tok_rows * lax.axis_size("head") // lengths.shape[0]
    own_sentences = tok_rows // span
    own_lengths = lax.dynamic_slice(lengths, (lax.axis_index("head") * own_sentences,), (own_sentences,))
    read = row_ids % span < jnp.repeat(own_lengths, span)
    hits = ((hit0 | hit1) & read[:, None]).astype(bf16)
    earlier = (row_ids[:, None] > row_ids[None, :]).astype(bf16)
    prior = jnp.dot(earlier, hits, preferred_element_type=f32)

    there = prior[:, :, None] == jnp.asarray(SLOTS, f32)[None, None, :]
    placing = ((hits > 0)[:, :, None] & there).astype(bf16).reshape(tok_rows, -1)
    outgoing = spread(placing, normed).astype(bf16)
    arrived = exchange(outgoing, experts).reshape(-1, width)
    (top_places, bottom_places, rest_places), used = pack(arrived)
    top, bottom = select(top_places, arrived), select(bottom_places, arrived)
    is_last = (jnp.arange(ROOM[1], dtype=jnp.int32) == ROOM[1] - 1)[:, None]
    bottom = jnp.where(is_last, (used > sum(ROOM) - 1).astype(bf16), bottom)

    def rest_of(crowded):
        def some():
            blocks = ring_blocks(select(rest_places, arrived))
            return few_through_experts(blocks, expert_in, expert_out)

        return lax.cond(crowded, some, lambda: jnp.zeros((rest_places.shape[0], width), bf16))

    crowded = (used > sum(ROOM) - 1).astype(jnp.int32)
    top, bottom, rest = through_experts(top, bottom, crowded, rest_of, expert_in, expert_out)
    answer = spread(top_places, top) + spread(bottom_places, bottom) + spread(rest_places, rest)
    answer = answer.astype(bf16)
    answers = [(there, exchange(answer, experts).reshape(-1, width))]

    logits = jnp.dot(normed, router, preferred_element_type=f32)
    chosen0 = jnp.sum(jnp.where(hit0, logits, 0.0), axis=1)
    chosen1 = jnp.sum(jnp.where(hit1, logits, 0.0), axis=1)
    first = jax.nn.sigmoid(chosen0 - chosen1)
    second = 1.0 - first
    mixed_rows = xf
    for hit, gate in ((hit0, first), (hit1, second)):
        picked = 0.0
        for there, returned in answers:
            picking = (hit[:, :, None] & there).astype(bf16).reshape(tok_rows, -1)
            picked = picked + jnp.dot(picking, returned, preferred_element_type=f32)
        mixed_rows = mixed_rows + gate[:, None] * picked
    memory = norm_rows(mixed_rows, final_gain).astype(bf16)
    local_cols = w_key.shape[1]
    joined = jnp.concatenate([w_key, w_value], axis=1)
    half = tok_rows // 2
    top, bottom = memory[:half], memory[half:]
    left_top, right_bottom = shift(top, 1), shift(bottom, -1)
    left_bottom, right_top = shift(bottom, 1), shift(top, -1)
    far_top, far_bottom = shift(left_top, 1), shift(right_bottom, -1)
    me = lax.axis_index("head")
    ring = lax.axis_size("head")
    left, right, far = ((me + by) % ring * tok_rows for by in (ring - 1, 1, 2))
    projected = jnp.zeros((ring * tok_rows, 2 * local_cols), bf16)
    for rows, offset in (
        (memory, me * tok_rows),
        (left_top, left),
        (right_bottom, right + half),
        (left_bottom, left + half),
        (right_top, right),
        (far_top, far),
        (far_bottom, far + half),
    ):
        columns = jnp.dot(rows, joined, preferred_element_type=f32).astype(bf16)
        projected = lax.dynamic_update_slice(projected, columns, (offset, 0))
    keys = projected[:, :local_cols]
    values = projected[:, local_cols:]
    sentences = dec_state.shape[0]
    local_heads = local_cols // HD
    keys_split = keys.reshape(sentences, span, local_heads, HD)
    values_split = values.reshape(sentences, span, local_heads, HD)
    valid = jnp.arange(span, dtype=jnp.int32)[None, :] < lengths[:, None]
    state = dec_state
    results = []
    for step in range(STEPS):
        normed_state = norm_rows(state.astype(f32), dec_gain).astype(bf16)
        query = (
            (jnp.dot(normed_state, w_query, preferred_element_type=f32) * HD ** (-0.5))
            .astype(bf16)
            .reshape(sentences, local_heads, HD)
        )
        scores = jnp.einsum("shd,sthd->sht", query, keys_split, preferred_element_type=f32)
        scores = jnp.where(valid[:, None, :], scores, -1e30)
        top = jnp.max(scores, axis=2, keepdims=True)
        raised = jnp.exp(scores - top)
        probs = (raised / jnp.sum(raised, axis=2, keepdims=True)).astype(bf16)
        attended = (
            jnp.einsum("sht,sthd->shd", probs, values_split, preferred_element_type=f32)
            .astype(bf16)
            .reshape(sentences, local_cols)
        )
        partial_update = jnp.dot(attended, w_output, preferred_element_type=f32).astype(bf16)
        total_update = ring_sum(partial_update)
        state = (state.astype(f32) + total_update).astype(bf16)
        results.append(state)
    return jnp.stack(results)


def solution(mesh):
    in_specs = (
        P(("dp", "head"), None),
        P(("dp", "head"), None),
        P("dp"),
        P(),
        P(),
        P("dp", None, "head"),
        P("dp", "head", None),
        P(),
        P(None, "head"),
        P(None, "head"),
        P(None, "head"),
        P("head", None),
        P(),
        P("dp", None),
    )
    out_specs = P(None, "dp", None)
    return jax.shard_map(local, mesh=mesh, in_specs=in_specs, out_specs=out_specs, check_vma=False)
```

```python
import functools

import jax
import jax.numpy as jnp
from jax import lax
from jax.experimental import pallas as pl
from jax.experimental.pallas import tpu as pltpu
from jax.sharding import PartitionSpec as P

HD = 128
STEPS = 2
ROOM = (128, 112)
EPS = 1e-05
CAPACITY = 5


def norm_rows(rows, gain):
    mean = jnp.mean(rows, axis=-1, keepdims=True)
    centred = rows - mean
    spread = jnp.mean(centred * centred, axis=-1, keepdims=True)
    return centred * lax.rsqrt(spread + EPS) * gain


def shift(rows, by):
    n = lax.axis_size("head")
    return lax.ppermute(rows, "head", [(i, (i + by) % n) for i in range(n)])


def exchange(packed):
    return lax.all_to_all(packed, "dp", split_axis=0, concat_axis=0, tiled=True)


def hold_kernel(first, second, first_out, second_out, sems):
    copies = [
        pltpu.make_async_copy(first.at[0], first_out, sems.at[0]),
        pltpu.make_async_copy(second.at[0], second_out, sems.at[1]),
    ]
    for copy in copies:
        copy.start()
    for copy in copies:
        copy.wait()


def hold(first, second):
    return pl.pallas_call(
        hold_kernel,
        out_shape=[pltpu.VMEM(x.shape[1:], x.dtype) for x in (first, second)],
        in_specs=[pl.BlockSpec(memory_space=pltpu.HBM)] * 2,
        out_specs=[pl.BlockSpec(memory_space=pltpu.VMEM)] * 2,
        scratch_shapes=[pltpu.SemaphoreType.DMA((2,))],
        compiler_params=pltpu.CompilerParams(vmem_limit_bytes=24 << 20),
    )(first, second)


def ffn_kernel(count, *refs):
    ins, w_in, w_out, outs = refs[:count], refs[count], refs[count + 1], refs[count + 2 : 2 * count + 2]
    flag, rows = refs[2 * count + 2 :]
    at = 0
    for ref in ins:
        rows[at : at + ref.shape[0], :] = ref[...]
        at += ref.shape[0]
    last = rows[at - 16 : at, 0:128].astype(jnp.float32)
    is_last = lax.broadcasted_iota(jnp.int32, last.shape, 0) == 15
    flag[0, 0] = jnp.max(jnp.where(is_last, last, 0.0)).astype(jnp.int32)
    hidden = jnp.maximum(jnp.dot(rows[...], w_in[...], preferred_element_type=jnp.float32), 0.0).astype(jnp.bfloat16)
    shares = jnp.dot(hidden, w_out[...], preferred_element_type=jnp.float32).astype(jnp.bfloat16)
    at = 0
    for ref in outs:
        ref[...] = shares[at : at + ref.shape[0], :]
        at += ref.shape[0]


def ffn(blocks, w_in, w_out):
    width, units = w_in.shape
    total = sum(block.shape[0] for block in blocks)
    whole = pl.BlockSpec(memory_space=pltpu.VMEM)
    *shares, flag = pl.pallas_call(
        functools.partial(ffn_kernel, len(blocks)),
        out_shape=[jax.ShapeDtypeStruct(block.shape, jnp.bfloat16) for block in blocks]
        + [jax.ShapeDtypeStruct((1, 1), jnp.int32)],
        in_specs=[whole] * (len(blocks) + 2),
        out_specs=[whole] * len(blocks) + [pl.BlockSpec(memory_space=pltpu.SMEM)],
        scratch_shapes=[pltpu.VMEM((total, width), jnp.bfloat16)],
        compiler_params=pltpu.CompilerParams(vmem_limit_bytes=24 << 20),
        cost_estimate=pl.CostEstimate(
            flops=4 * total * width * units, bytes_accessed=4 * total * width, transcendentals=0
        ),
    )(*blocks, pltpu.with_memory_space_constraint(w_in, pltpu.VMEM), pltpu.with_memory_space_constraint(w_out, pltpu.VMEM))
    return shares, flag[0, 0]


def ring_blocks(rows):
    return [rows] + [shift(rows, by) for by in (1, -1, 2)]


def few_through_experts(blocks, expert_in, expert_out):
    shares, unused = ffn(blocks, expert_in, expert_out)
    total = shares[0].astype(jnp.float32)
    for share, by in zip(shares[1:], (-1, 1, -2)):
        total = total + shift(share, by).astype(jnp.float32)
    return total.astype(jnp.bfloat16)


def vmem_call(kernel, out_shape, *args, smem=(), smem_out=(), scratch=()):
    whole, scalars = pl.BlockSpec(memory_space=pltpu.VMEM), pl.BlockSpec(memory_space=pltpu.SMEM)
    return pl.pallas_call(
        kernel,
        out_shape=out_shape,
        in_specs=[scalars if i in smem else whole for i in range(len(args))],
        out_specs=[scalars if i in smem_out else whole for i in range(len(out_shape))],
        scratch_shapes=scratch,
        compiler_params=pltpu.CompilerParams(vmem_limit_bytes=24 << 20),
    )(*args)


def over_rows(left, right):
    return lax.dot_general(left, right, (((0,), (0,)), ((), ())), preferred_element_type=jnp.float32)


def ids(shape, axis):
    return lax.broadcasted_iota(jnp.int32, shape, axis)


def route_kernel(capacity, *refs):
    f32, bf16 = jnp.float32, jnp.bfloat16
    given, (outgoing, info), held, sems = refs[:5], refs[5:7], refs[7:12], refs[12]
    copies = [pltpu.make_async_copy(src, dst, sems.at[i]) for i, (src, dst) in enumerate(zip(given, held))]
    for copy in copies:
        copy.start()
    for copy in copies:
        copy.wait()
    tokens, routes, lengths, gain, router = held
    rows, width = tokens.shape
    experts = router.shape[0]
    ring = lax.axis_size("head")
    span = rows * ring // lengths.shape[0]
    own = rows // span
    normed = norm_rows(tokens[...].astype(f32), gain[...]).astype(bf16)
    row = ids((rows, 1), 0)
    read = row < 0
    for sentence in range(own):
        length = lengths[lax.axis_index("head") * own + sentence]
        read = read | ((row >= sentence * span) & (row < sentence * span + length))
    diagonal = ids((rows, rows), 0) == ids((rows, rows), 1)
    named = [
        jnp.sum(jnp.where(diagonal, routes[k : k + 1, :].astype(f32), 0.0), axis=1, keepdims=True) for k in (0, 1)
    ]
    expert = ids((rows, experts), 1).astype(f32)
    hit0, hit1 = named[0] == expert, named[1] == expert
    hits = jnp.where((hit0 | hit1) & read, 1.0, 0.0).astype(bf16)
    earlier = jnp.where(ids((rows, rows), 0) > ids((rows, rows), 1), 1.0, 0.0).astype(bf16)
    prior = jnp.dot(earlier, hits, preferred_element_type=f32)
    logits = lax.dot_general(normed, router[...], (((1,), (1,)), ((), ())), preferred_element_type=f32)
    places, chosen = [], []
    for k, hit in ((0, hit0), (1, hit1)):
        slot = jnp.sum(jnp.where(hit, prior, 0.0), axis=1, keepdims=True)
        place = named[k] * capacity + slot
        places.append(jnp.where(read, place, -1.0))
        chosen.append(jnp.sum(jnp.where(hit, logits, 0.0), axis=1, keepdims=True))
    first = jax.nn.sigmoid(chosen[0] - chosen[1])
    slots = ids((rows, experts * capacity), 1).astype(f32)
    placing = jnp.where((places[0] == slots) | (places[1] == slots), 1.0, 0.0).astype(bf16)
    outgoing[...] = over_rows(placing, normed).astype(bf16).reshape(outgoing.shape)
    column = ids((rows, 128), 1)
    info[...] = jnp.where(column == 0, places[0], jnp.where(column == 1, places[1], first))


def pack_kernel(arrived, top, bottom, places, crowded):
    f32, bf16 = jnp.float32, jnp.bfloat16
    width = top.shape[1]
    rows = arrived[...].reshape(-1, width)
    count = rows.shape[0]
    used = jnp.max(jnp.abs(rows.astype(f32)), axis=1, keepdims=True) > 0
    marks = jnp.broadcast_to(jnp.where(used, 1.0, 0.0), (count, 128)).astype(bf16)
    earlier = jnp.where(ids((count, count), 0) > ids((count, count), 1), 1.0, 0.0).astype(bf16)
    place = jnp.dot(earlier, marks, preferred_element_type=f32)[:, 0:1]
    total = jnp.sum(jnp.where(used, 1.0, 0.0))
    front = sum(ROOM) - 1
    column = ids(places.shape, 1)
    slot = jnp.where(column < front, column, jnp.where(column == front, -2, column - 1)).astype(f32)
    chosen = jnp.where(used & (place == slot), 1.0, 0.0).astype(bf16)
    places[...] = chosen
    packed = over_rows(chosen[:, : front + 1], rows).astype(bf16)
    top[...] = packed[: ROOM[0]]
    more = jnp.where(total > front, 1.0, 0.0)
    is_last = ids(bottom.shape, 0) == ROOM[1] - 1
    bottom[...] = jnp.where(is_last, more, packed[ROOM[0] :].astype(f32)).astype(bf16)
    crowded[0, 0] = more.astype(jnp.int32)


def unpack_kernel(own_top, a_top, b_top, own_bottom, a_bottom, b_bottom, rest, places, answer, rows):
    f32, bf16 = jnp.float32, jnp.bfloat16
    at = 0
    for terms in ((own_top, a_top, b_top), (own_bottom, a_bottom, b_bottom), (rest,)):
        size = terms[0].shape[0]
        rows[at : at + size, :] = functools.reduce(lambda a, b: a + b, [term[...].astype(f32) for term in terms]).astype(bf16)
        at += size
    spread = jnp.dot(places[...], rows[...], preferred_element_type=f32)
    answer[...] = spread.astype(bf16).reshape(answer.shape)


def mix_kernel(returned, info, tokens, gain, top, bottom):
    f32, bf16 = jnp.float32, jnp.bfloat16
    rows, width = tokens.shape
    answers = returned[...].reshape(-1, width)
    slots = ids((rows, answers.shape[0]), 1).astype(f32)
    facts = info[...]
    mixed = tokens[...].astype(f32)
    for place, gate in ((facts[:, 0:1], facts[:, 2:3]), (facts[:, 1:2], 1.0 - facts[:, 2:3])):
        picking = jnp.where(place == slots, 1.0, 0.0).astype(bf16)
        mixed = mixed + gate * jnp.dot(picking, answers, preferred_element_type=f32)
    memory = norm_rows(mixed, gain[...]).astype(bf16)
    top[...] = memory[: rows // 2]
    bottom[...] = memory[rows // 2 :]


def add(*terms):
    return functools.reduce(lambda a, b: a + b, [term.astype(jnp.float32) for term in terms]).astype(jnp.bfloat16)


def through_experts(top, bottom, crowded, rest_of, expert_in, expert_out):
    left_top, right_bottom = shift(top, 1), shift(bottom, -1)
    left_bottom, right_top = shift(bottom, 1), shift(top, -1)
    far_top, far_bottom = shift(left_top, 1), shift(right_bottom, -1)
    (for_left_top, for_right_bottom), flag1 = ffn((left_top, right_bottom), expert_in, expert_out)
    far_top, far_bottom, for_left_top, for_right_bottom = lax.optimization_barrier(
        (far_top, far_bottom, for_left_top, for_right_bottom)
    )
    (for_far_top, for_far_bottom), flag2 = ffn((far_top, far_bottom), expert_in, expert_out)
    passing_top, passing_bottom = shift(for_far_top, 1), shift(for_far_bottom, -1)
    right_top, left_bottom, for_far_top, for_far_bottom = lax.optimization_barrier(
        (right_top, left_bottom, for_far_top, for_far_bottom)
    )
    (for_right_top, for_left_bottom), flag3 = ffn((right_top, left_bottom), expert_in, expert_out)
    a_bottom, b_top = shift(for_right_bottom, 1), shift(for_left_top, -1)
    to_right, to_left = add(for_right_top, passing_top), add(for_left_bottom, passing_bottom)
    a_top, b_bottom = shift(to_right, 1), shift(to_left, -1)
    crowded, *unused = lax.optimization_barrier((crowded + flag1 + flag2 + flag3, to_right, to_left))
    rest = rest_of(crowded > 0)
    top, bottom, rest = lax.optimization_barrier((top, bottom, rest))
    (own_top, own_bottom), unused = ffn((top, bottom), expert_in, expert_out)
    return own_top, a_top, b_top, own_bottom, a_bottom, b_bottom, rest


def ring_sum(rows):
    f32 = jnp.float32
    others = [shift(rows, by) for by in (1, -1, 2)]
    total = rows.astype(f32)
    for other in others:
        total = total + other.astype(f32)
    return total


def local(
    tokens,
    routes,
    lengths,
    moe_gain,
    router,
    expert_in,
    expert_out,
    final_gain,
    w_query,
    w_key,
    w_value,
    w_output,
    dec_gain,
    dec_state,
):
    experts = lax.axis_size("dp")
    tok_rows, width = tokens.shape
    f32, bf16 = jnp.float32, jnp.bfloat16
    layout = (experts, CAPACITY * (width // 128), 128)
    given = (tokens, routes.T, lengths, moe_gain[None], router.T)
    outgoing, info = pl.pallas_call(
        functools.partial(route_kernel, CAPACITY),
        out_shape=[jax.ShapeDtypeStruct(layout, bf16), jax.ShapeDtypeStruct((tok_rows, 128), f32)],
        in_specs=[pl.BlockSpec(memory_space=pltpu.HBM)] * len(given),
        out_specs=[pl.BlockSpec(memory_space=pltpu.VMEM)] * 2,
        scratch_shapes=[
            (pltpu.SMEM if x is lengths else pltpu.VMEM)(x.shape, x.dtype) for x in given
        ] + [pltpu.SemaphoreType.DMA((len(given),))],
        compiler_params=pltpu.CompilerParams(vmem_limit_bytes=58 << 20),
    )(*given)
    arrived = exchange(outgoing)
    held = hold(expert_in, expert_out)
    arrived, *held = lax.optimization_barrier((arrived, *held))
    count = experts * CAPACITY
    rest_rows = -(-(count - sum(ROOM) + 1) // 16) * 16
    top, bottom, places, crowded = vmem_call(
        pack_kernel,
        [jax.ShapeDtypeStruct((size, width), bf16) for size in ROOM]
        + [jax.ShapeDtypeStruct((count, sum(ROOM) + rest_rows), bf16), jax.ShapeDtypeStruct((1, 1), jnp.int32)],
        arrived,
        smem_out=(3,),
    )

    def rest_of(crowded):
        def some():
            rest = over_rows(places[:, sum(ROOM) :], arrived.reshape(count, width)).astype(bf16)
            return few_through_experts(ring_blocks(rest), *hold(expert_in, expert_out))

        return lax.cond(crowded, some, lambda: jnp.zeros((rest_rows, width), bf16))

    terms = through_experts(top, bottom, crowded[0, 0], rest_of, *held)
    (answer,) = vmem_call(
        unpack_kernel,
        [jax.ShapeDtypeStruct(layout, bf16)],
        *terms, places,
        scratch=[pltpu.VMEM((sum(ROOM) + rest_rows, width), bf16)],
    )
    half = tok_rows // 2
    top, bottom = vmem_call(
        mix_kernel,
        [jax.ShapeDtypeStruct((half, width), bf16)] * 2,
        exchange(answer), info, tokens, final_gain[None],
    )
    local_cols = w_key.shape[1]
    joined = jnp.concatenate([w_key, w_value], axis=1)
    left_top, right_bottom = shift(top, 1), shift(bottom, -1)
    left_top, right_bottom, top, bottom = lax.optimization_barrier((left_top, right_bottom, top, bottom))
    far_top, far_bottom = shift(left_top, 1), shift(right_bottom, -1)
    left_bottom, right_top = shift(bottom, 1), shift(top, -1)
    me = lax.axis_index("head")
    ring = lax.axis_size("head")
    left, right, far = ((me + by) % ring * tok_rows for by in (ring - 1, 1, 2))
    projected = jnp.zeros((ring * tok_rows, 2 * local_cols), bf16)
    for rows, offset in (
        (top, me * tok_rows),
        (bottom, me * tok_rows + half),
        (left_top, left),
        (right_bottom, right + half),
        (left_bottom, left + half),
        (right_top, right),
        (far_top, far),
        (far_bottom, far + half),
    ):
        columns = jnp.dot(rows, joined, preferred_element_type=f32).astype(bf16)
        projected = lax.dynamic_update_slice(projected, columns, (offset, 0))
    keys = projected[:, :local_cols]
    values = projected[:, local_cols:]
    sentences = dec_state.shape[0]
    span = keys.shape[0] // sentences
    local_heads = local_cols // HD
    keys_split = keys.reshape(sentences, span, local_heads, HD)
    values_split = values.reshape(sentences, span, local_heads, HD)
    valid = jnp.arange(span, dtype=jnp.int32)[None, :] < lengths[:, None]
    state = dec_state
    results = []
    for step in range(STEPS):
        normed_state = norm_rows(state.astype(f32), dec_gain).astype(bf16)
        query = (
            (jnp.dot(normed_state, w_query, preferred_element_type=f32) * HD ** (-0.5))
            .astype(bf16)
            .reshape(sentences, local_heads, HD)
        )
        scores = jnp.einsum("shd,sthd->sht", query, keys_split, preferred_element_type=f32)
        scores = jnp.where(valid[:, None, :], scores, -1e30)
        top = jnp.max(scores, axis=2, keepdims=True)
        raised = jnp.exp(scores - top)
        probs = (raised / jnp.sum(raised, axis=2, keepdims=True)).astype(bf16)
        attended = (
            jnp.einsum("sht,sthd->shd", probs, values_split, preferred_element_type=f32)
            .astype(bf16)
            .reshape(sentences, local_cols)
        )
        partial_update = jnp.dot(attended, w_output, preferred_element_type=f32).astype(bf16)
        total_update = ring_sum(partial_update)
        state = (state.astype(f32) + total_update).astype(bf16)
        results.append(state)
    return jnp.stack(results)


def solution(mesh):
    in_specs = (
        P(("dp", "head"), None),
        P(("dp", "head"), None),
        P("dp"),
        P(),
        P(),
        P("dp", None, "head"),
        P("dp", "head", None),
        P(),
        P(None, "head"),
        P(None, "head"),
        P(None, "head"),
        P("head", None),
        P(),
        P("dp", None),
    )
    out_specs = P(None, "dp", None)
    return jax.shard_map(local, mesh=mesh, in_specs=in_specs, out_specs=out_specs, check_vma=False)
```

```python
import functools

import jax
import jax.numpy as jnp
from jax import lax
from jax.experimental import pallas as pl
from jax.experimental.pallas import tpu as pltpu
from jax.sharding import PartitionSpec as P

HD = 128
STEPS = 2
ROOM = (128, 112)
EPS = 1e-05
CAPACITY = 5


def norm_rows(rows, gain):
    mean = jnp.mean(rows, axis=-1, keepdims=True)
    centred = rows - mean
    spread = jnp.mean(centred * centred, axis=-1, keepdims=True)
    return centred * lax.rsqrt(spread + EPS) * gain


def shift(rows, by):
    n = lax.axis_size("head")
    return lax.ppermute(rows, "head", [(i, (i + by) % n) for i in range(n)])


def exchange(packed):
    return lax.all_to_all(packed, "dp", split_axis=0, concat_axis=0, tiled=True)


def hold_kernel(first, second, first_out, second_out, sems):
    copies = [
        pltpu.make_async_copy(first.at[0], first_out, sems.at[0]),
        pltpu.make_async_copy(second.at[0], second_out, sems.at[1]),
    ]
    for copy in copies:
        copy.start()
    for copy in copies:
        copy.wait()


def hold(first, second):
    return pl.pallas_call(
        hold_kernel,
        out_shape=[pltpu.VMEM(x.shape[1:], x.dtype) for x in (first, second)],
        in_specs=[pl.BlockSpec(memory_space=pltpu.HBM)] * 2,
        out_specs=[pl.BlockSpec(memory_space=pltpu.VMEM)] * 2,
        scratch_shapes=[pltpu.SemaphoreType.DMA((2,))],
        compiler_params=pltpu.CompilerParams(vmem_limit_bytes=24 << 20),
    )(first, second)


def ffn_kernel(count, *refs):
    ins, w_in, w_out, outs = refs[:count], refs[count], refs[count + 1], refs[count + 2 : 2 * count + 2]
    flag, rows = refs[2 * count + 2 :]
    at = 0
    for ref in ins:
        rows[at : at + ref.shape[0], :] = ref[...]
        at += ref.shape[0]
    last = rows[at - 16 : at, 0:128].astype(jnp.float32)
    is_last = lax.broadcasted_iota(jnp.int32, last.shape, 0) == 15
    flag[0, 0] = jnp.max(jnp.where(is_last, last, 0.0)).astype(jnp.int32)
    hidden = jnp.maximum(jnp.dot(rows[...], w_in[...], preferred_element_type=jnp.float32), 0.0).astype(jnp.bfloat16)
    shares = jnp.dot(hidden, w_out[...], preferred_element_type=jnp.float32).astype(jnp.bfloat16)
    at = 0
    for ref in outs:
        ref[...] = shares[at : at + ref.shape[0], :]
        at += ref.shape[0]


def ffn(blocks, w_in, w_out):
    width, units = w_in.shape
    total = sum(block.shape[0] for block in blocks)
    whole = pl.BlockSpec(memory_space=pltpu.VMEM)
    *shares, flag = pl.pallas_call(
        functools.partial(ffn_kernel, len(blocks)),
        out_shape=[jax.ShapeDtypeStruct(block.shape, jnp.bfloat16) for block in blocks]
        + [jax.ShapeDtypeStruct((1, 1), jnp.int32)],
        in_specs=[whole] * (len(blocks) + 2),
        out_specs=[whole] * len(blocks) + [pl.BlockSpec(memory_space=pltpu.SMEM)],
        scratch_shapes=[pltpu.VMEM((total, width), jnp.bfloat16)],
        compiler_params=pltpu.CompilerParams(vmem_limit_bytes=24 << 20),
        cost_estimate=pl.CostEstimate(
            flops=4 * total * width * units, bytes_accessed=4 * total * width, transcendentals=0
        ),
    )(*blocks, pltpu.with_memory_space_constraint(w_in, pltpu.VMEM), pltpu.with_memory_space_constraint(w_out, pltpu.VMEM))
    return shares, flag[0, 0]


def ring_blocks(rows):
    return [rows] + [shift(rows, by) for by in (1, -1, 2)]


def few_through_experts(blocks, expert_in, expert_out):
    shares, unused = ffn(blocks, expert_in, expert_out)
    total = shares[0].astype(jnp.float32)
    for share, by in zip(shares[1:], (-1, 1, -2)):
        total = total + shift(share, by).astype(jnp.float32)
    return total.astype(jnp.bfloat16)


def vmem_call(kernel, out_shape, *args, smem=(), smem_out=(), scratch=()):
    whole, scalars = pl.BlockSpec(memory_space=pltpu.VMEM), pl.BlockSpec(memory_space=pltpu.SMEM)
    return pl.pallas_call(
        kernel,
        out_shape=out_shape,
        in_specs=[scalars if i in smem else whole for i in range(len(args))],
        out_specs=[scalars if i in smem_out else whole for i in range(len(out_shape))],
        scratch_shapes=scratch,
        compiler_params=pltpu.CompilerParams(vmem_limit_bytes=24 << 20),
    )(*args)


def over_rows(left, right):
    return lax.dot_general(left, right, (((0,), (0,)), ((), ())), preferred_element_type=jnp.float32)


def ids(shape, axis):
    return lax.broadcasted_iota(jnp.int32, shape, axis)


def route_kernel(capacity, *refs):
    f32, bf16 = jnp.float32, jnp.bfloat16
    given, (outgoing, info), held, sems = refs[:5], refs[5:7], refs[7:12], refs[12]
    copies = [pltpu.make_async_copy(src, dst, sems.at[i]) for i, (src, dst) in enumerate(zip(given, held))]
    for copy in copies:
        copy.start()
    for copy in copies:
        copy.wait()
    tokens, routes, lengths, gain, router = held
    rows, width = tokens.shape
    experts = router.shape[0]
    ring = lax.axis_size("head")
    span = rows * ring // lengths.shape[0]
    own = rows // span
    normed = norm_rows(tokens[...].astype(f32), gain[...]).astype(bf16)
    row = ids((rows, 1), 0)
    read = row < 0
    for sentence in range(own):
        length = lengths[lax.axis_index("head") * own + sentence]
        read = read | ((row >= sentence * span) & (row < sentence * span + length))
    diagonal = ids((rows, rows), 0) == ids((rows, rows), 1)
    named = [
        jnp.sum(jnp.where(diagonal, routes[k : k + 1, :].astype(f32), 0.0), axis=1, keepdims=True) for k in (0, 1)
    ]
    expert = ids((rows, experts), 1).astype(f32)
    hit0, hit1 = named[0] == expert, named[1] == expert
    hits = jnp.where((hit0 | hit1) & read, 1.0, 0.0).astype(bf16)
    earlier = jnp.where(ids((rows, rows), 0) > ids((rows, rows), 1), 1.0, 0.0).astype(bf16)
    prior = jnp.dot(earlier, hits, preferred_element_type=f32)
    logits = lax.dot_general(normed, router[...], (((1,), (1,)), ((), ())), preferred_element_type=f32)
    places, chosen = [], []
    for k, hit in ((0, hit0), (1, hit1)):
        slot = jnp.sum(jnp.where(hit, prior, 0.0), axis=1, keepdims=True)
        place = named[k] * capacity + slot
        places.append(jnp.where(read, place, -1.0))
        chosen.append(jnp.sum(jnp.where(hit, logits, 0.0), axis=1, keepdims=True))
    first = jax.nn.sigmoid(chosen[0] - chosen[1])
    slots = ids((rows, experts * capacity), 1).astype(f32)
    placing = jnp.where((places[0] == slots) | (places[1] == slots), 1.0, 0.0).astype(bf16)
    outgoing[...] = over_rows(placing, normed).astype(bf16).reshape(outgoing.shape)
    column = ids((rows, 128), 1)
    info[...] = jnp.where(column == 0, places[0], jnp.where(column == 1, places[1], first))


def pack_kernel(arrived, top, bottom, places, crowded):
    f32, bf16 = jnp.float32, jnp.bfloat16
    width = top.shape[1]
    rows = arrived[...].reshape(-1, width)
    count = rows.shape[0]
    used = jnp.max(jnp.abs(rows.astype(f32)), axis=1, keepdims=True) > 0
    marks = jnp.broadcast_to(jnp.where(used, 1.0, 0.0), (count, 128)).astype(bf16)
    earlier = jnp.where(ids((count, count), 0) > ids((count, count), 1), 1.0, 0.0).astype(bf16)
    place = jnp.dot(earlier, marks, preferred_element_type=f32)[:, 0:1]
    total = jnp.sum(jnp.where(used, 1.0, 0.0))
    front = sum(ROOM) - 1
    column = ids(places.shape, 1)
    slot = jnp.where(column < front, column, jnp.where(column == front, -2, column - 1)).astype(f32)
    chosen = jnp.where(used & (place == slot), 1.0, 0.0).astype(bf16)
    places[...] = chosen
    packed = over_rows(chosen[:, : front + 1], rows).astype(bf16)
    top[...] = packed[: ROOM[0]]
    more = jnp.where(total > front, 1.0, 0.0)
    is_last = ids(bottom.shape, 0) == ROOM[1] - 1
    bottom[...] = jnp.where(is_last, more, packed[ROOM[0] :].astype(f32)).astype(bf16)
    crowded[0, 0] = more.astype(jnp.int32)


def unpack_kernel(own_top, a_top, b_top, own_bottom, a_bottom, b_bottom, rest, places, answer, rows):
    f32, bf16 = jnp.float32, jnp.bfloat16
    at = 0
    for terms in ((own_top, a_top, b_top), (own_bottom, a_bottom, b_bottom), (rest,)):
        size = terms[0].shape[0]
        rows[at : at + size, :] = functools.reduce(lambda a, b: a + b, [term[...].astype(f32) for term in terms]).astype(bf16)
        at += size
    spread = jnp.dot(places[...], rows[...], preferred_element_type=f32)
    answer[...] = spread.astype(bf16).reshape(answer.shape)


def mix_kernel(returned, info, tokens, gain, top, bottom):
    f32, bf16 = jnp.float32, jnp.bfloat16
    rows, width = tokens.shape
    answers = returned[...].reshape(-1, width)
    slots = ids((rows, answers.shape[0]), 1).astype(f32)
    facts = info[...]
    mixed = tokens[...].astype(f32)
    for place, gate in ((facts[:, 0:1], facts[:, 2:3]), (facts[:, 1:2], 1.0 - facts[:, 2:3])):
        picking = jnp.where(place == slots, 1.0, 0.0).astype(bf16)
        mixed = mixed + gate * jnp.dot(picking, answers, preferred_element_type=f32)
    memory = norm_rows(mixed, gain[...]).astype(bf16)
    top[...] = memory[: rows // 2]
    bottom[...] = memory[rows // 2 :]


def add(*terms):
    return functools.reduce(lambda a, b: a + b, [term.astype(jnp.float32) for term in terms]).astype(jnp.bfloat16)


def through_experts(top, bottom, crowded, rest_of, expert_in, expert_out):
    left_top, right_bottom = shift(top, 1), shift(bottom, -1)
    left_bottom, right_top = shift(bottom, 1), shift(top, -1)
    far_top, far_bottom = shift(left_top, 1), shift(right_bottom, -1)
    (for_left_top, for_right_bottom), flag1 = ffn((left_top, right_bottom), expert_in, expert_out)
    far_top, far_bottom, for_left_top, for_right_bottom = lax.optimization_barrier(
        (far_top, far_bottom, for_left_top, for_right_bottom)
    )
    (for_far_top, for_far_bottom), flag2 = ffn((far_top, far_bottom), expert_in, expert_out)
    passing_top, passing_bottom = shift(for_far_top, 1), shift(for_far_bottom, -1)
    right_top, left_bottom, for_far_top, for_far_bottom = lax.optimization_barrier(
        (right_top, left_bottom, for_far_top, for_far_bottom)
    )
    (for_right_top, for_left_bottom), flag3 = ffn((right_top, left_bottom), expert_in, expert_out)
    a_bottom, b_top = shift(for_right_bottom, 1), shift(for_left_top, -1)
    to_right, to_left = add(for_right_top, passing_top), add(for_left_bottom, passing_bottom)
    a_top, b_bottom = shift(to_right, 1), shift(to_left, -1)
    crowded, *unused = lax.optimization_barrier((crowded + flag1 + flag2 + flag3, to_right, to_left))
    rest = rest_of(crowded > 0)
    top, bottom, rest = lax.optimization_barrier((top, bottom, rest))
    (own_top, own_bottom), unused = ffn((top, bottom), expert_in, expert_out)
    return own_top, a_top, b_top, own_bottom, a_bottom, b_bottom, rest


def ring_sum(rows):
    n = lax.axis_size("head")
    others = [lax.ppermute(rows, "head", [(i, i ^ by) for i in range(n)]) for by in (1, 3, 2)]
    return functools.reduce(lambda a, b: a + b, [other.astype(jnp.float32) for other in others], rows.astype(jnp.float32))


def local(
    tokens,
    routes,
    lengths,
    moe_gain,
    router,
    expert_in,
    expert_out,
    final_gain,
    w_query,
    w_key,
    w_value,
    w_output,
    dec_gain,
    dec_state,
):
    experts = lax.axis_size("dp")
    tok_rows, width = tokens.shape
    f32, bf16 = jnp.float32, jnp.bfloat16
    layout = (experts, CAPACITY * (width // 128), 128)
    given = (tokens, routes.T, lengths, moe_gain[None], router.T)
    outgoing, info = pl.pallas_call(
        functools.partial(route_kernel, CAPACITY),
        out_shape=[jax.ShapeDtypeStruct(layout, bf16), jax.ShapeDtypeStruct((tok_rows, 128), f32)],
        in_specs=[pl.BlockSpec(memory_space=pltpu.HBM)] * len(given),
        out_specs=[pl.BlockSpec(memory_space=pltpu.VMEM)] * 2,
        scratch_shapes=[
            (pltpu.SMEM if x is lengths else pltpu.VMEM)(x.shape, x.dtype) for x in given
        ] + [pltpu.SemaphoreType.DMA((len(given),))],
        compiler_params=pltpu.CompilerParams(vmem_limit_bytes=58 << 20),
    )(*given)
    arrived = exchange(outgoing)
    held = hold(expert_in, expert_out)
    arrived, *held = lax.optimization_barrier((arrived, *held))
    count = experts * CAPACITY
    rest_rows = -(-(count - sum(ROOM) + 1) // 16) * 16
    top, bottom, places, crowded = vmem_call(
        pack_kernel,
        [jax.ShapeDtypeStruct((size, width), bf16) for size in ROOM]
        + [jax.ShapeDtypeStruct((count, sum(ROOM) + rest_rows), bf16), jax.ShapeDtypeStruct((1, 1), jnp.int32)],
        arrived,
        smem_out=(3,),
    )

    def rest_of(crowded):
        def some():
            rest = over_rows(places[:, sum(ROOM) :], arrived.reshape(count, width)).astype(bf16)
            return few_through_experts(ring_blocks(rest), *hold(expert_in, expert_out))

        return lax.cond(crowded, some, lambda: jnp.zeros((rest_rows, width), bf16))

    terms = through_experts(top, bottom, crowded[0, 0], rest_of, *held)
    (answer,) = vmem_call(
        unpack_kernel,
        [jax.ShapeDtypeStruct(layout, bf16)],
        *terms, places,
        scratch=[pltpu.VMEM((sum(ROOM) + rest_rows, width), bf16)],
    )
    half = tok_rows // 2
    top, bottom = vmem_call(
        mix_kernel,
        [jax.ShapeDtypeStruct((half, width), bf16)] * 2,
        exchange(answer), info, tokens, final_gain[None],
    )
    local_cols = w_key.shape[1]
    joined = jnp.concatenate([w_key, w_value], axis=1)
    left_top, right_bottom = shift(top, 1), shift(bottom, -1)
    left_top, right_bottom, top, bottom = lax.optimization_barrier((left_top, right_bottom, top, bottom))
    far_top, far_bottom = shift(left_top, 1), shift(right_bottom, -1)
    left_bottom, right_top = shift(bottom, 1), shift(top, -1)
    me = lax.axis_index("head")
    ring = lax.axis_size("head")
    left, right, far = ((me + by) % ring * tok_rows for by in (ring - 1, 1, 2))
    projected = jnp.zeros((ring * tok_rows, 2 * local_cols), bf16)
    for rows, offset in (
        (top, me * tok_rows),
        (bottom, me * tok_rows + half),
        (left_top, left),
        (right_bottom, right + half),
        (left_bottom, left + half),
        (right_top, right),
        (far_top, far),
        (far_bottom, far + half),
    ):
        columns = jnp.dot(rows, joined, preferred_element_type=f32).astype(bf16)
        projected = lax.dynamic_update_slice(projected, columns, (offset, 0))
    keys = projected[:, :local_cols]
    values = projected[:, local_cols:]
    sentences = dec_state.shape[0]
    span = keys.shape[0] // sentences
    local_heads = local_cols // HD
    keys_split = keys.reshape(sentences, span, local_heads, HD)
    values_split = values.reshape(sentences, span, local_heads, HD)
    valid = jnp.arange(span, dtype=jnp.int32)[None, :] < lengths[:, None]
    state = dec_state
    results = []
    for step in range(STEPS):
        normed_state = norm_rows(state.astype(f32), dec_gain).astype(bf16)
        query = (
            (jnp.dot(normed_state, w_query, preferred_element_type=f32) * HD ** (-0.5))
            .astype(bf16)
            .reshape(sentences, local_heads, HD)
        )
        scores = jnp.einsum("shd,sthd->sht", query, keys_split, preferred_element_type=f32)
        scores = jnp.where(valid[:, None, :], scores, -1e30)
        top = jnp.max(scores, axis=2, keepdims=True)
        raised = jnp.exp(scores - top)
        probs = (raised / jnp.sum(raised, axis=2, keepdims=True)).astype(bf16)
        attended = (
            jnp.einsum("sht,sthd->shd", probs, values_split, preferred_element_type=f32)
            .astype(bf16)
            .reshape(sentences, local_cols)
        )
        partial_update = jnp.dot(attended, w_output, preferred_element_type=f32).astype(bf16)
        total_update = ring_sum(partial_update)
        state = (state.astype(f32) + total_update).astype(bf16)
        results.append(state)
    return jnp.stack(results)


def solution(mesh):
    in_specs = (
        P(("dp", "head"), None),
        P(("dp", "head"), None),
        P("dp"),
        P(),
        P(),
        P("dp", None, "head"),
        P("dp", "head", None),
        P(),
        P(None, "head"),
        P(None, "head"),
        P(None, "head"),
        P("head", None),
        P(),
        P("dp", None),
    )
    out_specs = P(None, "dp", None)
    return jax.shard_map(local, mesh=mesh, in_specs=in_specs, out_specs=out_specs, check_vma=False)
```

```python
import functools

import jax
import jax.numpy as jnp
from jax import lax
from jax.experimental import pallas as pl
from jax.experimental.pallas import tpu as pltpu
from jax.sharding import PartitionSpec as P

HD = 128
STEPS = 2
ROOM = (128, 112)
EPS = 1e-05
CAPACITY = 5


def norm_rows(rows, gain):
    mean = jnp.mean(rows, axis=-1, keepdims=True)
    centred = rows - mean
    spread = jnp.mean(centred * centred, axis=-1, keepdims=True)
    return centred * lax.rsqrt(spread + EPS) * gain


def shift(rows, by):
    n = lax.axis_size("head")
    return lax.ppermute(rows, "head", [(i, (i + by) % n) for i in range(n)])


def exchange(packed):
    return lax.all_to_all(packed, "dp", split_axis=0, concat_axis=0, tiled=True)


def hold_kernel(first, second, first_out, second_out, sems):
    copies = [
        pltpu.make_async_copy(first.at[0], first_out, sems.at[0]),
        pltpu.make_async_copy(second.at[0], second_out, sems.at[1]),
    ]
    for copy in copies:
        copy.start()
    for copy in copies:
        copy.wait()


def hold(first, second):
    return pl.pallas_call(
        hold_kernel,
        out_shape=[pltpu.VMEM(x.shape[1:], x.dtype) for x in (first, second)],
        in_specs=[pl.BlockSpec(memory_space=pltpu.HBM)] * 2,
        out_specs=[pl.BlockSpec(memory_space=pltpu.VMEM)] * 2,
        scratch_shapes=[pltpu.SemaphoreType.DMA((2,))],
        compiler_params=pltpu.CompilerParams(vmem_limit_bytes=24 << 20),
    )(first, second)


def ffn_kernel(count, *refs):
    ins, w_in, w_out, given = refs[:count], refs[count], refs[count + 1], refs[count + 2]
    outs = refs[count + 3 : 2 * count + 3]
    flag, rows = refs[2 * count + 3 :]
    at = 0
    for ref in ins:
        rows[at : at + ref.shape[0], :] = ref[...]
        at += ref.shape[0]
    last = rows[at - 16 : at, 0:128].astype(jnp.float32)
    is_last = lax.broadcasted_iota(jnp.int32, last.shape, 0) == 15
    flag[0, 0] = given[0, 0] + jnp.max(jnp.where(is_last, last, 0.0)).astype(jnp.int32)
    hidden = jnp.maximum(jnp.dot(rows[...], w_in[...], preferred_element_type=jnp.float32), 0.0).astype(jnp.bfloat16)
    shares = jnp.dot(hidden, w_out[...], preferred_element_type=jnp.float32).astype(jnp.bfloat16)
    at = 0
    for ref in outs:
        ref[...] = shares[at : at + ref.shape[0], :]
        at += ref.shape[0]


def ffn(blocks, w_in, w_out, given):
    width, units = w_in.shape
    total = sum(block.shape[0] for block in blocks)
    whole = pl.BlockSpec(memory_space=pltpu.VMEM)
    *shares, flag = pl.pallas_call(
        functools.partial(ffn_kernel, len(blocks)),
        out_shape=[jax.ShapeDtypeStruct(block.shape, jnp.bfloat16) for block in blocks]
        + [jax.ShapeDtypeStruct((1, 1), jnp.int32)],
        in_specs=[whole] * (len(blocks) + 2) + [pl.BlockSpec(memory_space=pltpu.SMEM)],
        out_specs=[whole] * len(blocks) + [pl.BlockSpec(memory_space=pltpu.SMEM)],
        scratch_shapes=[pltpu.VMEM((total, width), jnp.bfloat16)],
        compiler_params=pltpu.CompilerParams(vmem_limit_bytes=24 << 20),
        cost_estimate=pl.CostEstimate(
            flops=4 * total * width * units, bytes_accessed=4 * total * width, transcendentals=0
        ),
    )(*blocks, pltpu.with_memory_space_constraint(w_in, pltpu.VMEM), pltpu.with_memory_space_constraint(w_out, pltpu.VMEM), given)
    return shares, flag


def ring_blocks(rows):
    return [rows] + [shift(rows, by) for by in (1, -1, 2)]


def few_through_experts(blocks, expert_in, expert_out):
    shares, unused = ffn(blocks, expert_in, expert_out, jnp.zeros((1, 1), jnp.int32))
    total = shares[0].astype(jnp.float32)
    for share, by in zip(shares[1:], (-1, 1, -2)):
        total = total + shift(share, by).astype(jnp.float32)
    return total.astype(jnp.bfloat16)


def vmem_call(kernel, out_shape, *args, smem=(), smem_out=(), scratch=()):
    whole, scalars = pl.BlockSpec(memory_space=pltpu.VMEM), pl.BlockSpec(memory_space=pltpu.SMEM)
    return pl.pallas_call(
        kernel,
        out_shape=out_shape,
        in_specs=[scalars if i in smem else whole for i in range(len(args))],
        out_specs=[scalars if i in smem_out else whole for i in range(len(out_shape))],
        scratch_shapes=scratch,
        compiler_params=pltpu.CompilerParams(vmem_limit_bytes=24 << 20),
    )(*args)


def over_rows(left, right):
    return lax.dot_general(left, right, (((0,), (0,)), ((), ())), preferred_element_type=jnp.float32)


def ids(shape, axis):
    return lax.broadcasted_iota(jnp.int32, shape, axis)


def route_kernel(capacity, *refs):
    f32, bf16 = jnp.float32, jnp.bfloat16
    given, (outgoing, info), held, sems = refs[:5], refs[5:7], refs[7:12], refs[12]
    copies = [pltpu.make_async_copy(src, dst, sems.at[i]) for i, (src, dst) in enumerate(zip(given, held))]
    for copy in copies:
        copy.start()
    for copy in copies:
        copy.wait()
    tokens, routes, lengths, gain, router = held
    rows, width = tokens.shape
    experts = router.shape[0]
    ring = lax.axis_size("head")
    span = rows * ring // lengths.shape[0]
    own = rows // span
    normed = norm_rows(tokens[...].astype(f32), gain[...]).astype(bf16)
    row = ids((rows, 1), 0)
    read = row < 0
    for sentence in range(own):
        length = lengths[lax.axis_index("head") * own + sentence]
        read = read | ((row >= sentence * span) & (row < sentence * span + length))
    diagonal = ids((rows, rows), 0) == ids((rows, rows), 1)
    named = [
        jnp.sum(jnp.where(diagonal, routes[k : k + 1, :].astype(f32), 0.0), axis=1, keepdims=True) for k in (0, 1)
    ]
    expert = ids((rows, experts), 1).astype(f32)
    hit0, hit1 = named[0] == expert, named[1] == expert
    hits = jnp.where((hit0 | hit1) & read, 1.0, 0.0).astype(bf16)
    earlier = jnp.where(ids((rows, rows), 0) > ids((rows, rows), 1), 1.0, 0.0).astype(bf16)
    prior = jnp.dot(earlier, hits, preferred_element_type=f32)
    logits = lax.dot_general(normed, router[...], (((1,), (1,)), ((), ())), preferred_element_type=f32)
    places, chosen = [], []
    for k, hit in ((0, hit0), (1, hit1)):
        slot = jnp.sum(jnp.where(hit, prior, 0.0), axis=1, keepdims=True)
        place = named[k] * capacity + slot
        places.append(jnp.where(read, place, -1.0))
        chosen.append(jnp.sum(jnp.where(hit, logits, 0.0), axis=1, keepdims=True))
    first = jax.nn.sigmoid(chosen[0] - chosen[1])
    slots = ids((rows, experts * capacity), 1).astype(f32)
    placing = jnp.where((places[0] == slots) | (places[1] == slots), 1.0, 0.0).astype(bf16)
    outgoing[...] = over_rows(placing, normed).astype(bf16).reshape(outgoing.shape)
    column = ids((rows, 128), 1)
    info[...] = jnp.where(column == 0, places[0], jnp.where(column == 1, places[1], first))


def pack_kernel(arrived, top, bottom, places, crowded):
    f32, bf16 = jnp.float32, jnp.bfloat16
    width = top.shape[1]
    rows = arrived[...].reshape(-1, width)
    count = rows.shape[0]
    used = jnp.max(jnp.abs(rows.astype(f32)), axis=1, keepdims=True) > 0
    marks = jnp.broadcast_to(jnp.where(used, 1.0, 0.0), (count, 128)).astype(bf16)
    earlier = jnp.where(ids((count, count), 0) > ids((count, count), 1), 1.0, 0.0).astype(bf16)
    place = jnp.dot(earlier, marks, preferred_element_type=f32)[:, 0:1]
    total = jnp.sum(jnp.where(used, 1.0, 0.0))
    front = sum(ROOM) - 1
    column = ids(places.shape, 1)
    slot = jnp.where(column < front, column, jnp.where(column == front, -2, column - 1)).astype(f32)
    chosen = jnp.where(used & (place == slot), 1.0, 0.0).astype(bf16)
    places[...] = chosen
    packed = over_rows(chosen[:, : front + 1], rows).astype(bf16)
    top[...] = packed[: ROOM[0]]
    more = jnp.where(total > front, 1.0, 0.0)
    is_last = ids(bottom.shape, 0) == ROOM[1] - 1
    bottom[...] = jnp.where(is_last, more, packed[ROOM[0] :].astype(f32)).astype(bf16)
    crowded[0, 0] = more.astype(jnp.int32)


def unpack_kernel(own_top, a_top, b_top, own_bottom, a_bottom, b_bottom, rest, places, answer, rows):
    f32, bf16 = jnp.float32, jnp.bfloat16
    at = 0
    for terms in ((own_top, a_top, b_top), (own_bottom, a_bottom, b_bottom), (rest,)):
        size = terms[0].shape[0]
        rows[at : at + size, :] = functools.reduce(lambda a, b: a + b, [term[...].astype(f32) for term in terms]).astype(bf16)
        at += size
    spread = jnp.dot(places[...], rows[...], preferred_element_type=f32)
    answer[...] = spread.astype(bf16).reshape(answer.shape)


def mix_kernel(returned, info, tokens, gain, top, bottom):
    f32, bf16 = jnp.float32, jnp.bfloat16
    rows, width = tokens.shape
    answers = returned[...].reshape(-1, width)
    slots = ids((rows, answers.shape[0]), 1).astype(f32)
    facts = info[...]
    mixed = tokens[...].astype(f32)
    for place, gate in ((facts[:, 0:1], facts[:, 2:3]), (facts[:, 1:2], 1.0 - facts[:, 2:3])):
        picking = jnp.where(place == slots, 1.0, 0.0).astype(bf16)
        mixed = mixed + gate * jnp.dot(picking, answers, preferred_element_type=f32)
    memory = norm_rows(mixed, gain[...]).astype(bf16)
    top[...] = memory[: rows // 2]
    bottom[...] = memory[rows // 2 :]


def add(*terms):
    return functools.reduce(lambda a, b: a + b, [term.astype(jnp.float32) for term in terms]).astype(jnp.bfloat16)


def through_experts(top, bottom, crowded, rest_of, expert_in, expert_out):
    left_top, right_bottom = shift(top, 1), shift(bottom, -1)
    left_bottom, right_top = shift(bottom, 1), shift(top, -1)
    far_top, far_bottom = shift(left_top, 1), shift(right_bottom, -1)
    (for_left_top, for_right_bottom), flag1 = ffn((left_top, right_bottom), expert_in, expert_out, crowded)
    far_top, far_bottom, for_left_top, for_right_bottom = lax.optimization_barrier(
        (far_top, far_bottom, for_left_top, for_right_bottom)
    )
    (for_far_top, for_far_bottom), flag2 = ffn((far_top, far_bottom), expert_in, expert_out, flag1)
    passing_top, passing_bottom = shift(for_far_top, 1), shift(for_far_bottom, -1)
    right_top, left_bottom, for_far_top, for_far_bottom = lax.optimization_barrier(
        (right_top, left_bottom, for_far_top, for_far_bottom)
    )
    (for_right_top, for_left_bottom), flag3 = ffn((right_top, left_bottom), expert_in, expert_out, flag2)
    a_bottom, b_top = shift(for_right_bottom, 1), shift(for_left_top, -1)
    to_right, to_left = add(for_right_top, passing_top), add(for_left_bottom, passing_bottom)
    a_top, b_bottom = shift(to_right, 1), shift(to_left, -1)
    crowded, *unused = lax.optimization_barrier((flag3, to_right, to_left))
    rest = rest_of(crowded[0, 0] > 0)
    top, bottom, rest = lax.optimization_barrier((top, bottom, rest))
    (own_top, own_bottom), unused = ffn((top, bottom), expert_in, expert_out, crowded)
    return own_top, a_top, b_top, own_bottom, a_bottom, b_bottom, rest


def ring_sum(rows):
    n = lax.axis_size("head")
    others = [lax.ppermute(rows, "head", [(i, i ^ by) for i in range(n)]) for by in (1, 3, 2)]
    return functools.reduce(lambda a, b: a + b, [other.astype(jnp.float32) for other in others], rows.astype(jnp.float32))


def local(
    tokens,
    routes,
    lengths,
    moe_gain,
    router,
    expert_in,
    expert_out,
    final_gain,
    w_query,
    w_key,
    w_value,
    w_output,
    dec_gain,
    dec_state,
):
    experts = lax.axis_size("dp")
    tok_rows, width = tokens.shape
    f32, bf16 = jnp.float32, jnp.bfloat16
    layout = (experts, CAPACITY * (width // 128), 128)
    given = (tokens, routes.T, lengths, moe_gain[None], router.T)
    outgoing, info = pl.pallas_call(
        functools.partial(route_kernel, CAPACITY),
        out_shape=[jax.ShapeDtypeStruct(layout, bf16), jax.ShapeDtypeStruct((tok_rows, 128), f32)],
        in_specs=[pl.BlockSpec(memory_space=pltpu.HBM)] * len(given),
        out_specs=[pl.BlockSpec(memory_space=pltpu.VMEM)] * 2,
        scratch_shapes=[
            (pltpu.SMEM if x is lengths else pltpu.VMEM)(x.shape, x.dtype) for x in given
        ] + [pltpu.SemaphoreType.DMA((len(given),))],
        compiler_params=pltpu.CompilerParams(vmem_limit_bytes=58 << 20),
    )(*given)
    arrived = exchange(outgoing)
    held = hold(expert_in, expert_out)
    arrived, *held = lax.optimization_barrier((arrived, *held))
    count = experts * CAPACITY
    rest_rows = -(-(count - sum(ROOM) + 1) // 16) * 16
    top, bottom, places, crowded = vmem_call(
        pack_kernel,
        [jax.ShapeDtypeStruct((size, width), bf16) for size in ROOM]
        + [jax.ShapeDtypeStruct((count, sum(ROOM) + rest_rows), bf16), jax.ShapeDtypeStruct((1, 1), jnp.int32)],
        arrived,
        smem_out=(3,),
    )

    def rest_of(crowded):
        def some():
            rest = over_rows(places[:, sum(ROOM) :], arrived.reshape(count, width)).astype(bf16)
            return few_through_experts(ring_blocks(rest), *hold(expert_in, expert_out))

        return lax.cond(crowded, some, lambda: jnp.zeros((rest_rows, width), bf16))

    terms = through_experts(top, bottom, crowded, rest_of, *held)
    (answer,) = vmem_call(
        unpack_kernel,
        [jax.ShapeDtypeStruct(layout, bf16)],
        *terms, places,
        scratch=[pltpu.VMEM((sum(ROOM) + rest_rows, width), bf16)],
    )
    half = tok_rows // 2
    top, bottom = vmem_call(
        mix_kernel,
        [jax.ShapeDtypeStruct((half, width), bf16)] * 2,
        exchange(answer), info, tokens, final_gain[None],
    )
    local_cols = w_key.shape[1]
    joined = jnp.concatenate([w_key, w_value], axis=1)
    left_top, right_bottom = shift(top, 1), shift(bottom, -1)
    left_top, right_bottom, top, bottom = lax.optimization_barrier((left_top, right_bottom, top, bottom))
    far_top, far_bottom = shift(left_top, 1), shift(right_bottom, -1)
    left_bottom, right_top = shift(bottom, 1), shift(top, -1)
    me = lax.axis_index("head")
    ring = lax.axis_size("head")
    left, right, far = ((me + by) % ring * tok_rows for by in (ring - 1, 1, 2))
    projected = jnp.zeros((ring * tok_rows, 2 * local_cols), bf16)
    for rows, offset in (
        (top, me * tok_rows),
        (bottom, me * tok_rows + half),
        (left_top, left),
        (right_bottom, right + half),
        (left_bottom, left + half),
        (right_top, right),
        (far_top, far),
        (far_bottom, far + half),
    ):
        columns = jnp.dot(rows, joined, preferred_element_type=f32).astype(bf16)
        projected = lax.dynamic_update_slice(projected, columns, (offset, 0))
    keys = projected[:, :local_cols]
    values = projected[:, local_cols:]
    sentences = dec_state.shape[0]
    span = keys.shape[0] // sentences
    local_heads = local_cols // HD
    keys_split = keys.reshape(sentences, span, local_heads, HD)
    values_split = values.reshape(sentences, span, local_heads, HD)
    valid = jnp.arange(span, dtype=jnp.int32)[None, :] < lengths[:, None]
    state = dec_state
    results = []
    for step in range(STEPS):
        normed_state = norm_rows(state.astype(f32), dec_gain).astype(bf16)
        query = (
            (jnp.dot(normed_state, w_query, preferred_element_type=f32) * HD ** (-0.5))
            .astype(bf16)
            .reshape(sentences, local_heads, HD)
        )
        scores = jnp.einsum("shd,sthd->sht", query, keys_split, preferred_element_type=f32)
        scores = jnp.where(valid[:, None, :], scores, -1e30)
        top = jnp.max(scores, axis=2, keepdims=True)
        raised = jnp.exp(scores - top)
        probs = (raised / jnp.sum(raised, axis=2, keepdims=True)).astype(bf16)
        attended = (
            jnp.einsum("sht,sthd->shd", probs, values_split, preferred_element_type=f32)
            .astype(bf16)
            .reshape(sentences, local_cols)
        )
        partial_update = jnp.dot(attended, w_output, preferred_element_type=f32).astype(bf16)
        total_update = ring_sum(partial_update)
        state = (state.astype(f32) + total_update).astype(bf16)
        results.append(state)
    return jnp.stack(results)


def solution(mesh):
    in_specs = (
        P(("dp", "head"), None),
        P(("dp", "head"), None),
        P("dp"),
        P(),
        P(),
        P("dp", None, "head"),
        P("dp", "head", None),
        P(),
        P(None, "head"),
        P(None, "head"),
        P(None, "head"),
        P("head", None),
        P(),
        P("dp", None),
    )
    out_specs = P(None, "dp", None)
    return jax.shard_map(local, mesh=mesh, in_specs=in_specs, out_specs=out_specs, check_vma=False)
```
